512 devices in a mesh: replica: 8 (over x, core), fsdp: 16 (over z), owner: 4 (over y).
Axes of the slice: x: 4, y: 4, z: 16, core: 2. Of those that a mesh axis runs over, the one named last changes fastest.
Arguments:
- replica_grads: bfloat16 [8, 2, 4, 1024, 4096], P('replica', None, None, 'fsdp', 'owner'), may hold values from -0.15625 to 0.15625
- owner_table: int32 [4, 8, 1], replicated, may hold values from 0 to 7; in each aligned block of 8 rows (0 to 7, 8 to 15, ..., all dimensions but the last counted through in order) at most 2 rows name the same one
- stats_left: float32 [8, 4, 2, 1024, 1024], P('replica', 'owner', None, 'fsdp'), may hold values from -6 to 6
- stats_right: float32 [8, 4, 2, 1024, 1024], P('replica', 'owner', None, 'fsdp'), may hold values from -6 to 6
- left_root: bfloat16 [8, 4, 2, 1024, 1024], P('replica', 'owner', None, 'fsdp'), may hold values from -2.5 to 2.5
- right_root: bfloat16 [8, 4, 2, 1024, 1024], P('replica', 'owner', None, 'fsdp'), may hold values from -2.5 to 2.5
Outputs:
- update: bfloat16 [2, 4, 1024, 4096], P(None, None, 'fsdp', 'owner')
- new_left: float32 [8, 4, 2, 1024, 1024], P('replica', 'owner', None, 'fsdp')
- new_right: float32 [8, 4, 2, 1024, 1024], P('replica', 'owner', None, 'fsdp')
The draws below stay inside these ranges and needn't reach their ends.
Inputs may be any that keep to these rules, and one draw needn't show every extreme that they name: `owner_table`: in each block column no group owns more than 2 of its 8 blocks, and some group owns exactly 2.
All inputs are finite; a program needn't handle non-finite values.
Results may differ from the reference program's by a relative error of at most 0.019.
Values may be sent and summed in bfloat16 or wider, within the bound.
No kernel may reach another device: no remote copies, remote signals or barrier semaphores. Data moves between devices by JAX's collectives and lax.ppermute only.
A program may use at most 64 MiB of HBM per device.

```python
import math
import jax
import jax.numpy as jnp
import numpy as np
from jax import lax

BS = 1024
DW = 4096
MATS = 2
BR = 4
BC = 4
SLOTS = 2
N_REPLICA = 8


def block_levels(stream_key, shape, cuts, low, top_value):
    factor_of = 1.0
    for position, shards_of in cuts:
        heights = jax.random.uniform(jax.random.fold_in(jax.random.fold_in(stream_key, 6), position), (shards_of,), jnp.float32, low / len(cuts), top_value / len(cuts))
        factor_of = factor_of * jnp.repeat(jnp.exp(heights), shape[position] // shards_of).reshape((-1,) + (1,) * (len(shape) - 1 - position))
    return factor_of


def deal_out(key, own, number, rows, number_of, top, reach, slope):
    sequence = jax.random.permutation(key, number_of)
    packed, common = shares(number_of, rows * top, reach, slope, True), shares(number_of, rows * top, reach, slope, False)
    places = jnp.arange(number_of)

    def named(lengths, offset_by):
        used = int((lengths > 0).sum())
        fixed = max(1, used // 4)
        shifted = fixed + (places - fixed + offset_by * (used - fixed)) % max(1, number_of - fixed)
        return jnp.zeros((number_of,), jnp.int32).at[sequence[jnp.where(places < fixed, places, shifted)]].set(jnp.asarray(lengths, jnp.int32))

    lengths = jnp.where(number % 4 == 0, named(packed, number // 4), named(common, number - number // 4 - 1))
    mixed = jax.random.permutation(jax.random.fold_in(own, 3), number_of)
    giver, sink = mixed[0:number_of // 2 * 2:2], mixed[1:number_of // 2 * 2:2]
    margin = jnp.minimum(lengths[giver] - 1, reach - lengths[sink]) // 2
    margin = jnp.where((giver == sequence[0]) | (sink == sequence[0]) | (lengths[sink] == 0), 0, jnp.maximum(margin, 0))
    shifted = jax.random.randint(jax.random.fold_in(own, 4), (number_of // 2,), 0, 1 << 20) % (margin + 1)
    lengths = lengths.at[giver].add(-shifted).at[sink].add(shifted)
    items = jnp.searchsorted(jnp.cumsum(lengths), jnp.arange(rows * top), side="right").astype(jnp.int32)
    table = items.reshape(top, rows).T
    table = table[jax.random.permutation(jax.random.fold_in(own, 1), rows)]
    offset_by = jax.random.randint(jax.random.fold_in(own, 2), (rows, 1), 0, top)
    return jnp.take_along_axis(table, (jnp.arange(top)[None, :] + offset_by) % top, axis=1)


def shares(count, total, most, skew, full):
    loads = [(1 << 20) // math.isqrt(standing ** skew) + 1 for standing in range(1, count + 1)]
    largest = most if full else min(most, max(-(-total // count), total * loads[0] // sum(loads)))
    least = 1 if total - largest >= count - 1 else 0
    counts, surplus = [largest] + [least] * (count - 1), total - largest - least * (count - 1)
    while surplus > 0:
        movable = [i for i in range(1, count) if counts[i] < largest] or [i for i in range(1, count) if counts[i] < most]
        pool, remaining = sum([loads[i] for i in movable]), surplus
        for i in movable:
            extra = min(most - counts[i], max(1, remaining * loads[i] // pool), surplus)
            counts[i] = counts[i] + extra
            surplus = surplus - extra
    return np.array(counts)


def gaussian(rng, dims, width, most, cuts=(), held_as=jnp.bfloat16):
    level = block_levels(rng, dims, cuts, -0.22, 0.18) if cuts else 1.0
    values = jax.random.normal(rng, dims, jnp.float32) * width * level
    return jnp.minimum(jnp.maximum(values, -most), most).astype(held_as)


def setup_inputs(seed: int = 0) -> dict:
    arg_keys = jax.random.split(jax.random.key(seed), 7)
    replica_grads = gaussian(arg_keys[0], (N_REPLICA, MATS, BR, BS, DW), 0.011, 0.15625, ((0, 8), (3, 16), (4, 4)))
    owner_table_keys = jax.random.split(jax.random.fold_in(arg_keys[1], 1), BC * (MATS * BR) // (MATS * BR))
    owner_table_turns = jax.random.permutation(jax.random.fold_in(arg_keys[1], 3), BC * (MATS * BR) // (MATS * BR))
    owner_table = jax.vmap(lambda own, number: deal_out(jax.random.fold_in(arg_keys[1], 2), own, number, MATS * BR, N_REPLICA, 1, SLOTS, 2))(owner_table_keys, owner_table_turns).reshape((BC, MATS * BR, 1))
    stats_left = gaussian(arg_keys[2], (N_REPLICA, BC, SLOTS, BS, BS), 1.0, 6.0, ((0, 8), (1, 4), (3, 16)), jnp.float32)
    stats_right = gaussian(arg_keys[3], (N_REPLICA, BC, SLOTS, BS, BS), 1.0, 6.0, ((0, 8), (1, 4), (3, 16)), jnp.float32)
    left_root = gaussian(arg_keys[4], (N_REPLICA, BC, SLOTS, BS, BS), 0.18, 2.5, ((0, 8), (1, 4), (3, 16)))
    right_root = gaussian(arg_keys[5], (N_REPLICA, BC, SLOTS, BS, BS), 0.18, 2.5, ((0, 8), (1, 4), (3, 16)))
    return {"replica_grads": replica_grads, "owner_table": owner_table, "stats_left": stats_left, "stats_right": stats_right, "left_root": left_root, "right_root": right_root}


def slot_onehot(column, replicas, slot_count):
    length = column.shape[0]
    matching = column[:, None] == column[None, :]
    earlier = jnp.arange(length)[None, :] < jnp.arange(length)[:, None]
    slot_index = jnp.sum(jnp.logical_and(matching, earlier).astype(jnp.int32), axis=1)
    owners_hit = column[None, None, :] == jnp.arange(replicas, dtype=jnp.int32)[:, None, None]
    slots_hit = slot_index[None, None, :] == jnp.arange(slot_count, dtype=jnp.int32)[None, :, None]
    return jnp.logical_and(owners_hit, slots_hit).astype(jnp.float32)


def reference(replica_grads, owner_table, stats_left, stats_right, left_root, right_root):
    highest = lax.Precision.HIGHEST
    reduced = jnp.sum(replica_grads.astype(jnp.float32), axis=0)
    blocks = reduced.astype(jnp.bfloat16).reshape(MATS * BR, BS, BC, BS).transpose(2, 0, 1, 3)
    onehot = jax.vmap(lambda entries: slot_onehot(entries, N_REPLICA, SLOTS))(owner_table[:, :, 0])
    placed = jnp.einsum('crsq,cqij->rcsij', onehot, blocks.astype(jnp.float32), precision=highest).astype(jnp.bfloat16)
    widened = placed.astype(jnp.float32)
    new_left = stats_left + jnp.einsum('rcsik,rcsjk->rcsij', widened, widened, precision=highest)
    new_right = stats_right + jnp.einsum('rcski,rcskj->rcsij', widened, widened, precision=highest)
    product = jnp.einsum('rcsik,rcskj->rcsij', left_root.astype(jnp.float32), widened, precision=highest).astype(jnp.bfloat16)
    result = jnp.einsum('rcsik,rcskj->rcsij', product.astype(jnp.float32), right_root.astype(jnp.float32), precision=highest).astype(jnp.bfloat16)
    restored = jnp.einsum('crsq,rcsij->cqij', onehot, result.astype(jnp.float32), precision=highest).astype(jnp.bfloat16)
    update = restored.transpose(1, 2, 0, 3).reshape(MATS, BR, BS, DW)
    return (update, new_left, new_right)
```

```python
import jax
import jax.numpy as jnp
from jax import lax
from jax.experimental import pallas as pl
from jax.experimental.pallas import tpu as pltpu
from jax.sharding import Mesh, PartitionSpec as P

F32 = jnp.float32
BF16 = jnp.bfloat16
CORE_SWAP = ((0, 1), (1, 0))
VMEM = pl.BlockSpec(memory_space=pltpu.VMEM)
SMEM = pl.BlockSpec(memory_space=pltpu.SMEM)
PARAMS = pltpu.CompilerParams(vmem_limit_bytes=24 << 20)


def owner_and_slot(table_ref, column, q, blocks):
    owner = table_ref[column, q]
    slot = jnp.int32(0)
    for other in range(blocks):
        same = jnp.logical_and(table_ref[column, other] == owner, other < q)
        slot = slot + same.astype(jnp.int32)
    return owner, slot


def pack_kernel(table_ref, grads_ref, right_ref, left_ref, own_ref, sib_ref, own_left_ref, sib_left_ref):
    column = lax.axis_index("y")
    core = lax.axis_index("core")
    me = lax.axis_index("x") * 2 + core
    blocks = grads_ref.shape[0]
    for chip in range(own_ref.shape[0]):
        for parity, out_ref, out_left_ref in (
            (core, own_ref, own_left_ref),
            (1 - core, sib_ref, sib_left_ref),
        ):
            q = 2 * chip + parity
            out_ref[chip, 0] = grads_ref[q]
            owner, slot = owner_and_slot(table_ref, column, q, blocks)

            @pl.when(owner == me)
            def _():
                out_ref[chip, 1] = right_ref[slot]
                out_left_ref[chip] = left_ref[slot]

            @pl.when(owner != me)
            def _():
                out_ref[chip, 1] = jnp.zeros(right_ref.shape[1:], right_ref.dtype)
                out_left_ref[chip] = jnp.zeros(left_ref.shape[1:], left_ref.dtype)


def pack(table, grads, right, left, chips):
    rows, width = grads.shape[1:]
    pair = jax.ShapeDtypeStruct((chips, 2, rows, width), grads.dtype)
    single = jax.ShapeDtypeStruct((chips, rows, width), left.dtype)
    return pl.pallas_call(
        pack_kernel,
        out_shape=(pair, pair, single, single),
        in_specs=[SMEM, VMEM, VMEM, VMEM],
        out_specs=(VMEM,) * 4,
        compiler_params=PARAMS,
        name="pack",
    )(table, grads, right, left)


def unpack_kernel(table_ref, stats_left_ref, stats_right_ref, *refs):
    pieces, (update_ref, new_left_ref, new_right_ref) = refs[:-3], refs[-3:]
    column = lax.axis_index("y")
    core = lax.axis_index("core")
    x = lax.axis_index("x")
    me = x * 2 + core
    blocks = update_ref.shape[0]
    chips = blocks // 2
    new_left_ref[...] = stats_left_ref[...]
    new_right_ref[...] = stats_right_ref[...]
    for place, piece_ref in enumerate(pieces):
        chip = lax.rem(x - place // 2 + chips, chips)
        parity = core if place % 2 == 0 else 1 - core
        q = chip * 2 + parity
        update_ref[q] = piece_ref[0]
        owner, slot = owner_and_slot(table_ref, column, q, blocks)

        @pl.when(owner == me)
        def _():
            new_left_ref[slot] = stats_left_ref[slot] + piece_ref[1].astype(F32)
            new_right_ref[slot] = stats_right_ref[slot] + piece_ref[2].astype(F32)


def unpack(table, stats_left, stats_right, pieces, blocks):
    rows, width = pieces[0].shape[1:]
    stats = jax.ShapeDtypeStruct(stats_left.shape, stats_left.dtype)
    return pl.pallas_call(
        unpack_kernel,
        out_shape=(jax.ShapeDtypeStruct((blocks, rows, width), BF16), stats, stats),
        in_specs=[SMEM] + [VMEM] * (2 + len(pieces)),
        out_specs=(VMEM,) * 3,
        compiler_params=PARAMS,
        name="unpack",
    )(table, stats_left, stats_right, *pieces)


def route(own, sibling):
    swapped = lax.ppermute(sibling, "core", CORE_SWAP)
    pair = (own.astype(F32) + swapped.astype(F32)).astype(BF16)
    arrived = lax.all_to_all(pair, "x", split_axis=0, concat_axis=0, tiled=True)
    return jnp.sum(arrived, axis=0, dtype=F32).astype(BF16)


def local(replica_grads, owner_table, stats_left, stats_right, left_root, right_root):
    local_grads = replica_grads[0]
    matrices, rows_blocks, rows, width = local_grads.shape
    chips = lax.axis_size("x")
    blocks = matrices * rows_blocks
    table = owner_table[:, :, 0]
    own, sibling, own_left, sibling_left = pack(
        table, local_grads.reshape(blocks, rows, width), right_root[0, 0], left_root[0, 0], chips
    )
    strips = route(own, sibling)
    whole = lax.all_gather(strips, "z", axis=1, tiled=True)
    own_left, sibling_left, strips = lax.optimization_barrier((own_left, sibling_left, strips))
    left_strip = route(own_left, sibling_left)
    whole_block, whole_right = whole[0], whole[1]
    product = jnp.dot(left_strip, whole_block, preferred_element_type=F32).astype(BF16)
    result = jnp.dot(product, whole_right, preferred_element_type=F32).astype(BF16)
    left_term = jnp.einsum("ik,jk->ij", strips[0], whole_block, preferred_element_type=F32)
    own_cols = lax.dynamic_slice_in_dim(whole_block, lax.axis_index("z") * rows, rows, 1)
    right_term = jnp.einsum("ki,kj->ij", own_cols, whole_block, preferred_element_type=F32)
    payload = jnp.stack([result, left_term.astype(BF16), right_term.astype(BF16)])
    pieces = []
    for step in range(chips):
        piece = payload
        if step:
            piece = lax.ppermute(payload, "x", [(i, (i + step) % chips) for i in range(chips)])
        pieces += [piece, lax.ppermute(piece, "core", CORE_SWAP)]
    update, new_left, new_right = unpack(table, stats_left[0, 0], stats_right[0, 0], pieces, blocks)
    return (
        update.reshape(matrices, rows_blocks, rows, width),
        new_left[None, None],
        new_right[None, None],
    )


def solution(mesh):
    replicas, shards, columns = mesh.devices.shape
    split = Mesh(
        mesh.devices.reshape(replicas // 2, 2, shards, columns), ("x", "core", "z", "y")
    )
    replica = ("x", "core")
    owned = P(replica, "y", None, "z", None)
    return jax.shard_map(
        local,
        mesh=split,
        in_specs=(P(replica, None, None, "z", "y"), P(), owned, owned, owned, owned),
        out_specs=(P(None, None, "z", "y"), owned, owned),
        check_vma=False,
    )
```

```python
import jax
import jax.numpy as jnp
from jax import lax
from jax.experimental import pallas as pl
from jax.experimental.pallas import tpu as pltpu
from jax.sharding import Mesh, PartitionSpec as P

F32 = jnp.float32
BF16 = jnp.bfloat16
F16 = jnp.float16
CORE_SWAP = ((0, 1), (1, 0))
VMEM = pl.BlockSpec(memory_space=pltpu.VMEM)
SMEM = pl.BlockSpec(memory_space=pltpu.SMEM)
PARAMS = pltpu.CompilerParams(vmem_limit_bytes=24 << 20)


def owner_and_slot(table_ref, column, q, blocks):
    owner = table_ref[column, q]
    slot = jnp.int32(0)
    for other in range(blocks):
        same = jnp.logical_and(table_ref[column, other] == owner, other < q)
        slot = slot + same.astype(jnp.int32)
    return owner, slot


def pack_kernel(table_ref, grads_ref, right_ref, left_ref, own_ref, sib_ref, places_ref):
    column = lax.axis_index("y")
    core = lax.axis_index("core")
    me = lax.axis_index("x") * 2 + core
    blocks = grads_ref.shape[0]
    for i in range(places_ref.shape[0]):
        places_ref[i] = jnp.int32(0)
    for chip in range(own_ref.shape[0]):
        for parity, out_ref in ((core, own_ref), (1 - core, sib_ref)):
            q = 2 * chip + parity
            out_ref[chip, 0] = grads_ref[q]
            owner, slot = owner_and_slot(table_ref, column, q, blocks)

            @pl.when(owner == me)
            def _():
                out_ref[chip, 1] = right_ref[slot]
                out_ref[chip, 2] = left_ref[slot]
                places_ref[2 * slot] = q
                places_ref[2 * slot + 1] = jnp.int32(1)

            @pl.when(owner != me)
            def _():
                out_ref[chip, 1:] = jnp.zeros((2,) + right_ref.shape[1:], right_ref.dtype)


def pack(table, grads, right, left, chips):
    rows, width = grads.shape[1:]
    shape = jax.ShapeDtypeStruct((chips, 3, rows, width), grads.dtype)
    return pl.pallas_call(
        pack_kernel,
        out_shape=(shape, shape, jax.ShapeDtypeStruct((2 * right.shape[0],), jnp.int32)),
        in_specs=[SMEM, VMEM, VMEM, VMEM],
        out_specs=(VMEM, VMEM, SMEM),
        compiler_params=PARAMS,
        name="pack",
    )(table, grads, right, left)


def route(own, sibling):
    swapped = lax.ppermute(sibling, "core", CORE_SWAP)
    pair = (own.astype(F32) + swapped.astype(F32)).astype(BF16)
    arrived = lax.all_to_all(pair, "x", split_axis=0, concat_axis=0, tiled=True)
    return jnp.sum(arrived, axis=0, dtype=F32).astype(BF16)


def gather(strips, axis):
    count = len(strips)
    rows, width = strips[0].shape
    wide = jnp.stack([strip.astype(F32) for strip in strips])
    top = jnp.maximum(jnp.max(jnp.abs(wide), axis=(1, 2), keepdims=True), 1e-30)
    power = jnp.floor(jnp.log2(top)) - 13.0
    scaled = (wide * jnp.exp2(-power)).astype(F16).reshape(count * rows, width)
    powers = jnp.zeros((8, width), F16)
    for i in range(count):
        powers = jnp.where(lax.broadcasted_iota(jnp.int32, (8, width), 0) == i, power[i].astype(F16), powers)
    sent = jnp.concatenate([scaled, powers])
    got = lax.all_gather(sent, axis, axis=0, tiled=False)
    factor = jnp.exp2(got[:, count * rows : count * rows + count, :1].astype(F32))
    return [
        got[:, i * rows : (i + 1) * rows].astype(F32) * factor[:, i : i + 1] for i in range(count)
    ]


def local(replica_grads, owner_table, stats_left, stats_right, left_root, right_root):
    local_grads = replica_grads[0]
    matrices, rows_blocks, rows, width = local_grads.shape
    chips = lax.axis_size("x")
    blocks = matrices * rows_blocks
    table = owner_table[:, :, 0]
    own, sibling, places = pack(
        table, local_grads.reshape(blocks, rows, width), right_root[0, 0], left_root[0, 0], chips
    )
    block_strip, right_strip, left_strip = route(own, sibling)
    whole_block, whole_right = gather([block_strip, right_strip], "z")
    whole_block = whole_block.astype(BF16).reshape(-1, width)
    whole_right = whole_right.astype(BF16).reshape(-1, width)
    product = jnp.dot(left_strip, whole_block, preferred_element_type=F32).astype(BF16)
    result = jnp.dot(product, whole_right, preferred_element_type=F32).astype(BF16)
    left_term = jnp.einsum("ik,jk->ij", block_strip, whole_block, preferred_element_type=F32)
    own_cols = lax.dynamic_slice_in_dim(whole_block, lax.axis_index("z") * rows, rows, 1)
    right_term = jnp.einsum("ki,kj->ij", own_cols, whole_block, preferred_element_type=F32)
    updates, left_terms, right_terms = gather([result, left_term, right_term], ("x", "core"))
    update = updates.astype(BF16)
    new_left, new_right = [], []
    for slot in range(stats_left.shape[2]):
        place, owned = places[2 * slot], places[2 * slot + 1] > 0
        for terms, stats, new in ((left_terms, stats_left, new_left), (right_terms, stats_right, new_right)):
            term = lax.dynamic_index_in_dim(terms, place, 0, keepdims=False)
            new.append(stats[0, 0, slot] + jnp.where(owned, term, 0.0))
    new_left, new_right = jnp.stack(new_left), jnp.stack(new_right)
    return (
        update.reshape(matrices, rows_blocks, rows, width),
        new_left[None, None],
        new_right[None, None],
    )


def solution(mesh):
    replicas, shards, columns = mesh.devices.shape
    split = Mesh(
        mesh.devices.reshape(replicas // 2, 2, shards, columns), ("x", "core", "z", "y")
    )
    replica = ("x", "core")
    owned = P(replica, "y", None, "z", None)
    return jax.shard_map(
        local,
        mesh=split,
        in_specs=(P(replica, None, None, "z", "y"), P(), owned, owned, owned, owned),
        out_specs=(P(None, None, "z", "y"), owned, owned),
        check_vma=False,
    )
```

```python
import jax
import jax.numpy as jnp
from jax import lax
from jax.experimental import pallas as pl
from jax.experimental.pallas import tpu as pltpu
from jax.sharding import Mesh, PartitionSpec as P

F16 = jnp.float16
BF16 = jnp.bfloat16
F32 = jnp.float32
CORE_SWAP = ((0, 1), (1, 0))
VMEM = pl.BlockSpec(memory_space=pltpu.VMEM)
SMEM = pl.BlockSpec(memory_space=pltpu.SMEM)
PARAMS = pltpu.CompilerParams(vmem_limit_bytes=8 << 20)
POWER_ROWS = 8


def owner_and_slot(table_ref, column, q):
    owner = table_ref[column, q]
    slot = jnp.int32(0)
    for other in range(table_ref.shape[1]):
        same = jnp.logical_and(table_ref[column, other] == owner, other < q)
        slot = slot + same.astype(jnp.int32)
    return owner, slot


def pack_kernel(table_ref, grads_ref, right_root_ref, left_root_ref, swapped_ref, main_ref, places_ref):
    column = lax.axis_index("y")
    core = lax.axis_index("core")
    me = lax.axis_index("x") * 2 + core
    chips = main_ref.shape[0]
    slots = places_ref.shape[0] // 2
    for i in range(places_ref.shape[0]):
        places_ref[i] = jnp.int32(0)
    for q in range(2 * chips):
        owner, slot = owner_and_slot(table_ref, column, q)

        @pl.when(owner == me)
        def _():
            places_ref[2 * slot] = jnp.int32(q)
            places_ref[2 * slot + 1] = jnp.int32(1)

    for chip in range(chips):
        q = 2 * chip + core
        main_ref[chip, 0] = (grads_ref[q].astype(F32) + swapped_ref[chip].astype(F32)).astype(BF16)
        owner, slot = owner_and_slot(table_ref, column, q)

        @pl.when(owner == me)
        def _():
            main_ref[chip, 1] = right_root_ref[slot]
            main_ref[chip, 2] = left_root_ref[slot]

        @pl.when(owner == me + 1 - 2 * core)
        def _():
            main_ref[chip, 1] = swapped_ref[chips + slot]
            main_ref[chip, 2] = swapped_ref[chips + slots + slot]

        @pl.when(lax.shift_right_logical(owner, 1) != lax.axis_index("x"))
        def _():
            main_ref[chip, 1:] = jnp.zeros((2,) + main_ref.shape[2:], BF16)


def pack(table, grads, right, left, swapped, chips):
    rows, width = grads.shape[1:]
    slots = right.shape[0]
    return pl.pallas_call(
        pack_kernel,
        out_shape=(
            jax.ShapeDtypeStruct((chips, 3, rows, width), BF16),
            jax.ShapeDtypeStruct((2 * slots,), jnp.int32),
        ),
        in_specs=[SMEM] + [VMEM] * 4,
        out_specs=(VMEM, SMEM),
        compiler_params=PARAMS,
        name="pack",
    )(table, grads, right, left, swapped)


def put_scaled(out_ref, index, strip):
    rows, width = strip.shape
    top = jnp.max(jnp.max(jnp.abs(strip), axis=0, keepdims=True), axis=1, keepdims=True)
    power = jnp.floor(jnp.log2(jnp.maximum(top, 1e-30))) - 13.0
    out_ref[pl.ds(index * rows, rows), :] = strip * jnp.exp2(-power)
    return jnp.broadcast_to(power, (POWER_ROWS, width))


def put_powers(out_ref, powers):
    row = lax.broadcasted_iota(jnp.int32, (POWER_ROWS, out_ref.shape[1]), 0)
    block = powers[0]
    for i, power in enumerate(powers):
        block = jnp.where(row == i, power, block)
    out_ref[pl.ds(out_ref.shape[0] - POWER_ROWS, POWER_ROWS), :] = block


def scale_kernel(*refs):
    powers = [put_scaled(refs[-1], i, ref[...].astype(F32)) for i, ref in enumerate(refs[:-1])]
    put_powers(refs[-1], powers)


def scale_in_kernel(strips):
    rows, width = strips[0].shape
    return pl.pallas_call(
        scale_kernel,
        out_shape=jax.ShapeDtypeStruct((len(strips) * rows + POWER_ROWS, width), F32),
        in_specs=[VMEM] * len(strips),
        out_specs=VMEM,
        compiler_params=PARAMS,
        name="scale",
    )(*strips)


def scale(strips):
    rows, width = strips[0].shape
    wide = jnp.stack([strip.astype(F32) for strip in strips])
    top = jnp.maximum(jnp.max(jnp.abs(wide), axis=(1, 2), keepdims=True), 1e-30)
    power = jnp.floor(jnp.log2(top)) - 13.0
    scaled = (wide * jnp.exp2(-power)).astype(F16).reshape(len(strips) * rows, width)
    row = lax.broadcasted_iota(jnp.int32, (POWER_ROWS, width), 0)
    powers = jnp.zeros((POWER_ROWS, width), F16)
    for i in range(len(strips)):
        powers = jnp.where(row == i, power[i].astype(F16), powers)
    return jnp.concatenate([scaled, powers])


def gather(scaled, count, axis):
    got = lax.all_gather(scaled.astype(F16), axis, axis=0, tiled=False)
    body = got.shape[1] - POWER_ROWS
    rows = body // count
    factor = jnp.exp2(got[:, body : body + count, :1].astype(F32))
    return [
        got[:, i * rows : (i + 1) * rows].astype(F32) * factor[:, i : i + 1] for i in range(count)
    ]


def local(replica_grads, owner_table, stats_left, stats_right, left_root, right_root):
    local_grads = replica_grads[0]
    matrices, rows_blocks, rows, width = local_grads.shape
    chips = lax.axis_size("x")
    slots = stats_left.shape[2]
    blocks = matrices * rows_blocks
    grads = local_grads.reshape(blocks, rows, width)
    right, left = right_root[0, 0], left_root[0, 0]
    sibling = lax.dynamic_index_in_dim(
        grads.reshape(chips, 2, rows, width), 1 - lax.axis_index("core"), 1, keepdims=False
    )
    swapped = lax.ppermute(jnp.concatenate([sibling, right, left]), "core", CORE_SWAP)
    main, places = pack(owner_table[:, :, 0], grads, right, left, swapped, chips)
    arrived = lax.all_to_all(main, "x", split_axis=0, concat_axis=0, tiled=True)
    strips = jnp.sum(arrived, axis=0, dtype=F32).astype(BF16)
    scaled = scale([strips[0], strips[1]])
    whole_block, whole_right = gather(scaled, 2, "z")
    left_strip = strips[2]
    whole_block = whole_block.astype(BF16).reshape(-1, width)
    whole_right = whole_right.astype(BF16).reshape(-1, width)
    product = jnp.dot(left_strip, whole_block, preferred_element_type=F32).astype(BF16)
    result = jnp.dot(product, whole_right, preferred_element_type=F32).astype(BF16)
    left_term = jnp.einsum("ik,jk->ij", strips[0], whole_block, preferred_element_type=F32)
    own_cols = lax.dynamic_slice_in_dim(whole_block, lax.axis_index("z") * rows, rows, 1)
    right_term = jnp.einsum("ki,kj->ij", own_cols, whole_block, preferred_element_type=F32)
    updates, left_terms, right_terms = gather(
        scale_in_kernel([result, left_term, right_term]), 3, ("x", "core")
    )
    update = updates.astype(BF16)
    new_left, new_right = [], []
    for slot in range(slots):
        place, owned = places[2 * slot], places[2 * slot + 1] > 0
        for terms, stats, new in (
            (left_terms, stats_left, new_left),
            (right_terms, stats_right, new_right),
        ):
            term = lax.dynamic_index_in_dim(terms, place, 0, keepdims=False)
            new.append(stats[0, 0, slot] + jnp.where(owned, term, 0.0))
    return (
        update.reshape(matrices, rows_blocks, rows, width),
        jnp.stack(new_left)[None, None],
        jnp.stack(new_right)[None, None],
    )


def solution(mesh):
    replicas, shards, columns = mesh.devices.shape
    split = Mesh(
        mesh.devices.reshape(replicas // 2, 2, shards, columns), ("x", "core", "z", "y")
    )
    replica = ("x", "core")
    owned = P(replica, "y", None, "z", None)
    return jax.shard_map(
        local,
        mesh=split,
        in_specs=(P(replica, None, None, "z", "y"), P(), owned, owned, owned, owned),
        out_specs=(P(None, None, "z", "y"), owned, owned),
        check_vma=False,
    )
```

```python
import jax
import jax.numpy as jnp
from jax import lax
from jax.experimental import pallas as pl
from jax.experimental.pallas import tpu as pltpu
from jax.sharding import Mesh, PartitionSpec as P

F16 = jnp.float16
BF16 = jnp.bfloat16
F32 = jnp.float32
CORE_SWAP = ((0, 1), (1, 0))
VMEM = pl.BlockSpec(memory_space=pltpu.VMEM)
SMEM = pl.BlockSpec(memory_space=pltpu.SMEM)
PARAMS = pltpu.CompilerParams(vmem_limit_bytes=16 << 20)
POWER_ROWS = 8


def owner_and_slot(table_ref, column, q):
    owner = table_ref[column, q]
    slot = jnp.int32(0)
    for other in range(table_ref.shape[1]):
        same = jnp.logical_and(table_ref[column, other] == owner, other < q)
        slot = slot + same.astype(jnp.int32)
    return owner, slot


def pack_kernel(table_ref, grads_ref, right_root_ref, left_root_ref, swapped_ref, main_ref):
    column = lax.axis_index("y")
    core = lax.axis_index("core")
    me = lax.axis_index("x") * 2 + core
    chips = main_ref.shape[0]
    slots = right_root_ref.shape[0]
    for chip in range(chips):
        q = 2 * chip + core
        main_ref[chip, 0] = (grads_ref[q].astype(F32) + swapped_ref[chip].astype(F32)).astype(BF16)
        owner, slot = owner_and_slot(table_ref, column, q)

        @pl.when(owner == me)
        def _():
            main_ref[chip, 1] = right_root_ref[slot]
            main_ref[chip, 2] = left_root_ref[slot]

        @pl.when(owner == me + 1 - 2 * core)
        def _():
            main_ref[chip, 1] = swapped_ref[chips + slot]
            main_ref[chip, 2] = swapped_ref[chips + slots + slot]

        @pl.when(lax.shift_right_logical(owner, 1) != lax.axis_index("x"))
        def _():
            main_ref[chip, 1:] = jnp.zeros((2,) + main_ref.shape[2:], BF16)


def pack(table, grads, right, left, swapped, chips):
    rows, width = grads.shape[1:]
    return pl.pallas_call(
        pack_kernel,
        out_shape=jax.ShapeDtypeStruct((chips, 3, rows, width), BF16),
        in_specs=[SMEM] + [VMEM] * 4,
        out_specs=VMEM,
        compiler_params=PARAMS,
        name="pack",
    )(table, grads, right, left, swapped)


def statistics_kernel(table_ref, *refs):
    column = lax.axis_index("y")
    me = lax.axis_index("x") * 2 + lax.axis_index("core")
    for terms_ref, stats_ref, new_ref in zip(refs[:2], refs[2:4], refs[4:]):
        new_ref[...] = stats_ref[...]
        for q in range(terms_ref.shape[0]):
            owner, slot = owner_and_slot(table_ref, column, q)

            @pl.when(owner == me)
            def _():
                new_ref[slot] = stats_ref[slot] + terms_ref[q]


def statistics(table, terms, stats):
    shape = jax.ShapeDtypeStruct(stats[0].shape, F32)
    return pl.pallas_call(
        statistics_kernel,
        out_shape=(shape, shape),
        in_specs=[SMEM] + [VMEM] * 4,
        out_specs=(VMEM, VMEM),
        compiler_params=PARAMS,
        name="statistics",
    )(table, *terms, *stats)


def put_scaled(out_ref, index, strip):
    rows, width = strip.shape
    top = jnp.max(jnp.max(jnp.abs(strip), axis=0, keepdims=True), axis=1, keepdims=True)
    power = jnp.floor(jnp.log2(jnp.maximum(top, 1e-30))) - 13.0
    out_ref[pl.ds(index * rows, rows), :] = strip * jnp.exp2(-power)
    return jnp.broadcast_to(power, (POWER_ROWS, width))


def put_powers(out_ref, powers):
    row = lax.broadcasted_iota(jnp.int32, (POWER_ROWS, out_ref.shape[1]), 0)
    block = powers[0]
    for i, power in enumerate(powers):
        block = jnp.where(row == i, power, block)
    out_ref[pl.ds(out_ref.shape[0] - POWER_ROWS, POWER_ROWS), :] = block


def scale_kernel(*refs):
    powers = [put_scaled(refs[-1], i, ref[...].astype(F32)) for i, ref in enumerate(refs[:-1])]
    put_powers(refs[-1], powers)


def scale_in_kernel(strips):
    rows, width = strips[0].shape
    return pl.pallas_call(
        scale_kernel,
        out_shape=jax.ShapeDtypeStruct((len(strips) * rows + POWER_ROWS, width), F32),
        in_specs=[VMEM] * len(strips),
        out_specs=VMEM,
        compiler_params=PARAMS,
        name="scale",
    )(*strips)


def scale(strips):
    rows, width = strips[0].shape
    wide = jnp.stack([strip.astype(F32) for strip in strips])
    top = jnp.maximum(jnp.max(jnp.abs(wide), axis=(1, 2), keepdims=True), 1e-30)
    power = jnp.floor(jnp.log2(top)) - 13.0
    scaled = (wide * jnp.exp2(-power)).reshape(len(strips) * rows, width)
    powers = jnp.broadcast_to(power[:, 0], (len(strips), width))
    powers = jnp.pad(powers, ((0, POWER_ROWS - len(strips)), (0, 0)))
    return jnp.concatenate([scaled, powers])


def gather(scaled, count, axis):
    got = lax.all_gather(scaled.astype(F16), axis, axis=0, tiled=False)
    body = got.shape[1] - POWER_ROWS
    rows = body // count
    factor = jnp.exp2(got[:, body : body + count, :1].astype(F32))
    return [
        got[:, i * rows : (i + 1) * rows].astype(F32) * factor[:, i : i + 1] for i in range(count)
    ]


def local(replica_grads, owner_table, stats_left, stats_right, left_root, right_root):
    local_grads = replica_grads[0]
    matrices, rows_blocks, rows, width = local_grads.shape
    chips = lax.axis_size("x")
    blocks = matrices * rows_blocks
    grads = local_grads.reshape(blocks, rows, width)
    right, left = right_root[0, 0], left_root[0, 0]
    even, odd = grads.reshape(chips, 2, rows, width).transpose(1, 0, 2, 3)
    sibling = jnp.where(lax.axis_index("core") == 0, odd, even)
    swapped = lax.ppermute(jnp.concatenate([sibling, right, left]), "core", CORE_SWAP)
    table = owner_table[:, :, 0]
    main = pack(table, grads, right, left, swapped, chips)
    arrived = lax.all_to_all(main, "x", split_axis=0, concat_axis=0, tiled=True)
    strips = jnp.sum(arrived, axis=0, dtype=F32).astype(BF16)
    scaled = scale([strips[0], strips[1]])
    whole_block, whole_right = gather(scaled, 2, "z")
    left_strip = strips[2]
    whole_block = whole_block.astype(BF16).reshape(-1, width)
    whole_right = whole_right.astype(BF16).reshape(-1, width)
    product = jnp.dot(left_strip, whole_block, preferred_element_type=F32).astype(BF16)
    result = jnp.dot(product, whole_right, preferred_element_type=F32).astype(BF16)
    left_term = jnp.einsum("ik,jk->ij", strips[0], whole_block, preferred_element_type=F32)
    own_cols = lax.dynamic_slice_in_dim(whole_block, lax.axis_index("z") * rows, rows, 1)
    right_term = jnp.einsum("ki,kj->ij", own_cols, whole_block, preferred_element_type=F32)
    updates, left_terms, right_terms = gather(
        scale_in_kernel([result, left_term, right_term]), 3, ("x", "core")
    )
    update = updates.astype(BF16)
    new_left, new_right = statistics(
        table, (left_terms, right_terms), (stats_left[0, 0], stats_right[0, 0])
    )
    return (
        update.reshape(matrices, rows_blocks, rows, width),
        new_left[None, None],
        new_right[None, None],
    )


def solution(mesh):
    replicas, shards, columns = mesh.devices.shape
    split = Mesh(
        mesh.devices.reshape(replicas // 2, 2, shards, columns), ("x", "core", "z", "y")
    )
    replica = ("x", "core")
    owned = P(replica, "y", None, "z", None)
    return jax.shard_map(
        local,
        mesh=split,
        in_specs=(P(replica, None, None, "z", "y"), P(), owned, owned, owned, owned),
        out_specs=(P(None, None, "z", "y"), owned, owned),
        check_vma=False,
    )
```
